32 devices in a mesh: groups: 2 (over y), pool: 4 (over x, core), tp: 4 (over z).
Axes of the slice: x: 2, y: 2, z: 4, core: 2. Of those that a mesh axis runs over, the one named last changes fastest.
Arguments:
- inputs: bfloat16 [4, 1024, 8192], P(None, ('groups', 'pool'), 'tp'), parts along dimension 1, may hold values from -6 to 6
- out_weight: bfloat16 [8192, 8192], P('tp'), may hold values from -0.0625 to 0.0625
- shrink_store: bfloat16 [128, 64, 8192], P(('groups', 'pool'), None, 'tp'), parts along dimension 0, may hold values from -0.0625 to 0.0625
- expand_store: bfloat16 [128, 64, 8192], P(('groups', 'pool'), None, 'tp'), parts along dimension 0, may hold values from -0.75 to 0.75
- owner_map: int32 [128], P('groups'), parts along dimension 0, may hold values from 0 to 63, as said below
- requests: int32 [4, 8, 8], P(None, ('groups', 'pool')), parts along dimension 1, may hold values from 0 to 63, as said below
- row_slot: int32 [4, 1024], P(None, ('groups', 'pool')), parts along dimension 1, may hold values from 0 to 7
Outputs:
- projected: bfloat16 [4, 1024, 8192], P(None, ('groups', 'pool'), 'tp'), parts along dimension 1
The draws below stay inside these ranges and needn't reach their ends.
There are 2 independent parts, one for each index of `groups`. The reference program is written for one: setup_inputs(seed, part) draws one part's arguments, and reference() takes and returns one part's arrays. A program takes and returns all parts, laid end to end along the dimension named above; an argument that names none is the same for every part. Nothing has to cross between parts.
Inputs may be any that keep to these rules, and one draw needn't show every extreme that they name: `owner_map`: A permutation: each adapter id has its own store position; position q is held by pool index q // 16. `requests`: each list names 8 distinct adapter ids; at most 2 of them are stored on one pool index, and exactly 2 on some pool index in every list.
All inputs are finite; a program needn't handle non-finite values.
Results may differ from the reference program's by a relative error of at most 0.0047.
Values may be sent and summed in bfloat16 or wider, within the bound.
A program may use at most 192 MiB of HBM per device.

```python
import jax
import jax.numpy as jnp
from jax import lax

D = 8192
R = 64
ROWS = 128
STEPS = 4
SLOTS = 8
CAP = 2
ADP_DEV = 16
ADAPTERS = 64
N_POOL = 4


def shared_order(key):
    return jax.random.permutation(jax.random.fold_in(key, 11), ADAPTERS).astype(jnp.int32)


def owner_ranks(owners):
    count = owners.shape[-1]
    same = owners[..., :, None] == owners[..., None, :]
    earlier = jnp.arange(count)[:, None] < jnp.arange(count)[None, :]
    return jnp.sum((same & earlier).astype(jnp.int32), axis=-2)


def draw_owner_map(key, part):
    order = shared_order(key)
    return order


def draw_requests(key, part):
    order = shared_order(key)
    key = jax.random.fold_in(key, 5)
    inverse = jnp.zeros((ADAPTERS,), jnp.int32).at[order].set(jnp.arange(ADAPTERS, dtype=jnp.int32))

    def one_list(list_key):
        key_hot, key_rest, key_shuffle, key_local = jax.random.split(list_key, 4)
        hot_owner = jax.random.randint(key_hot, (), 0, N_POOL)
        copies = (jax.random.permutation(key_rest, N_POOL * CAP) // CAP).astype(jnp.int32)
        placing = jnp.argsort((copies == hot_owner).astype(jnp.int32), stable=True)
        rest = copies[placing]
        owners = jnp.concatenate([jnp.full((CAP,), hot_owner, jnp.int32), rest[:SLOTS - CAP]])
        owners = owners[jax.random.permutation(key_shuffle, SLOTS)]
        ranks = owner_ranks(owners)
        local_order = jax.random.permutation(key_local, ADP_DEV).astype(jnp.int32)
        local = local_order[(ranks + owners * CAP) % ADP_DEV]
        return inverse[owners * ADP_DEV + local]
    list_keys = jax.random.split(key, STEPS * N_POOL)
    return jax.vmap(one_list)(list_keys).reshape(STEPS, N_POOL, SLOTS).astype(jnp.int32)


def with_ends(entries, stream_key, least, high):
    longest = entries.shape.index(max(entries.shape))
    spots = []
    for shift in (0, 1):
        where = [jax.random.randint(jax.random.fold_in(stream_key, axis), (), 0, length) for axis, length in enumerate(entries.shape)]
        where[longest] = (where[longest] + shift) % entries.shape[longest]
        spots.append(tuple(where))
    return entries.at[spots[0]].set(least).at[spots[1]].set(high)


def levels(rng, extent, shards, low, top_value):
    def one(dim, blocks):
        draws = jax.random.uniform(jax.random.fold_in(jax.random.fold_in(rng, 6), dim), (blocks,), jnp.float32, low / len(shards), top_value / len(shards))
        return jnp.repeat(jnp.exp(draws), extent[dim] // blocks).reshape((-1,) + (1,) * (len(extent) - dim - 1))

    loudness = one(*shards[0])
    for cut in shards[1:]:
        loudness = loudness * one(*cut)
    return loudness


def gaussian(key, extent, scale, limit, cuts=(), kind=jnp.bfloat16):
    drawn = jax.random.normal(key, extent, jnp.float32) * scale
    if len(cuts) > 0:
        drawn = levels(key, extent, cuts, -0.22, 0.18) * drawn
    return jnp.clip(drawn, min=-limit, max=limit).astype(kind)


def setup_inputs(seed: int = 0, part: int = 0) -> dict:
    seeds = jax.random.split(jax.random.key(seed), 8)
    part_splits = jax.random.split(jax.random.fold_in(seeds[7], part), 8)
    inputs = gaussian(part_splits[0], (STEPS, N_POOL * ROWS, D), 1.0, 6.0, ((1, 4), (2, 4)))
    out_weight = gaussian(seeds[1], (D, D), D ** -0.5, 0.0625, ((0, 4),))
    shrink_store = gaussian(part_splits[2], (ADAPTERS, R, D), D ** -0.5, 0.0625, ((0, 4), (2, 4)))
    expand_store = gaussian(part_splits[3], (ADAPTERS, R, D), R ** -0.5, 0.75, ((0, 4), (2, 4)))
    owner_map = draw_owner_map(jax.random.fold_in(jax.random.fold_in(seeds[7], part), 71), part)
    requests = draw_requests(jax.random.fold_in(jax.random.fold_in(seeds[7], part), 71), part)
    row_slot = with_ends(jax.random.randint(part_splits[6], (STEPS, N_POOL * ROWS), 0, SLOTS), jax.random.fold_in(part_splits[6], 1), 0, SLOTS - 1).astype(jnp.int32)
    return {"inputs": inputs, "out_weight": out_weight, "shrink_store": shrink_store, "expand_store": expand_store, "owner_map": owner_map, "requests": requests, "row_slot": row_slot}


adapter_scale = 2.0


def one_replica(inputs_rows, request_ids, slot_rows, out_weight, shrink_store, expand_store, owner_map):
    token_positions = owner_map[request_ids]
    shrink_all = shrink_store[token_positions].reshape(SLOTS * R, D)
    expand_all = expand_store[token_positions].reshape(SLOTS * R, D)
    codes = lax.dot_general(inputs_rows, shrink_all, (((1,), (1,)), ((), ())), preferred_element_type=jnp.float32)
    onehot = (slot_rows[:, None] == jnp.arange(SLOTS, dtype=jnp.int32)[None, :]).astype(jnp.float32)
    chosen = jnp.sum(codes.reshape(ROWS, SLOTS, R) * onehot[:, :, None], axis=1).astype(jnp.bfloat16)
    spread = (onehot.astype(jnp.bfloat16)[:, :, None] * chosen[:, None, :]).reshape(ROWS, SLOTS * R)
    adapter_delta = jnp.dot(spread, expand_all, preferred_element_type=jnp.float32)
    frozen_base = jnp.dot(inputs_rows, out_weight, preferred_element_type=jnp.float32)
    return (frozen_base + adapter_scale * adapter_delta).astype(jnp.bfloat16)


def reference(inputs, out_weight, shrink_store, expand_store, owner_map, requests, row_slot):
    flat_inputs = inputs.reshape(STEPS * N_POOL, ROWS, D)
    flat_requests = requests.reshape(STEPS * N_POOL, SLOTS)
    flat_slots = row_slot.reshape(STEPS * N_POOL, ROWS)

    def apply_one(items):
        return one_replica(items[0], items[1], items[2], out_weight, shrink_store, expand_store, owner_map)

    result = lax.map(apply_one, (flat_inputs, flat_requests, flat_slots))
    return result.reshape(STEPS, N_POOL * ROWS, D)
```

```python
import functools

import jax
import jax.numpy as jnp
from jax import lax
from jax.experimental import pallas as pl
from jax.experimental.pallas import tpu as pltpu
from jax.sharding import PartitionSpec as P

adapter_scale = 2.0
LANES = 128
HALVES = 2


def lane_parts(shape, rank):
    lane = lax.broadcasted_iota(jnp.int32, shape, 1)
    return lane // rank, lane < rank


def shrink_kernel(count, rank, *refs):
    rows_refs = refs[:count]
    place_ref, store_ref, out_ref = refs[count:]
    block = store_ref.shape[0]
    length = rows_refs[0].shape[0]
    step = pl.program_id(0)
    part, low = lane_parts((length, LANES), rank)
    per_group = LANES // rank
    first = step * (block // rank)
    for pair in range(count // 2):
        folded = []
        for side in range(2):
            index = 2 * pair + side
            place = place_ref[pl.ds(index * length, length), :] - first
            codes = lax.dot_general(
                rows_refs[index][...],
                store_ref[...],
                (((1,), (1,)), ((), ())),
                preferred_element_type=jnp.float32,
            )
            picked = jnp.zeros((length, LANES), jnp.float32)
            for group in range(block // LANES):
                picked += jnp.where(
                    part + group * per_group == place,
                    codes[:, group * LANES : (group + 1) * LANES],
                    0.0,
                )
            folded.append(picked + pltpu.roll(picked, rank, 1))
        packed = jnp.where(low, folded[0], folded[1])
        where_to = pl.ds(pair * length, length)

        @pl.when(step == 0)
        def _():
            out_ref[where_to, :] = packed

        @pl.when(step > 0)
        def _():
            out_ref[where_to, :] += packed


def shrink(rows, places, store, rank):
    count, (length, features) = len(rows), rows[0].shape
    width = store.shape[0]
    block = min(256, width)
    whole = lambda array: pl.BlockSpec(array.shape, lambda i: (0, 0))
    out = jax.ShapeDtypeStruct((count // 2 * length, LANES), jnp.float32)
    return pl.pallas_call(
        functools.partial(shrink_kernel, count, rank),
        grid=(width // block,),
        in_specs=[whole(r) for r in rows]
        + [whole(places), pl.BlockSpec((block, features), lambda i: (i, 0))],
        out_specs=whole(out),
        out_shape=out,
        compiler_params=pltpu.CompilerParams(
            dimension_semantics=("arbitrary",), vmem_limit_bytes=40 * 2**20
        ),
        cost_estimate=pl.CostEstimate(
            flops=2 * count * length * features * width,
            bytes_accessed=2 * features * (count * length + width),
            transcendentals=0,
        ),
        name="shrink",
    )(*rows, places, store)


def expand_kernel(count, rank, place_ref, code_ref, store_ref, *out_refs):
    width = store_ref.shape[0]
    length = out_refs[0].shape[0]
    part, low = lane_parts((length, LANES), rank)
    per_group = LANES // rank
    for pair in range(count // 2):
        code = code_ref[pl.ds(pair * length, length), :].astype(jnp.bfloat16).astype(jnp.float32)
        turned = pltpu.roll(code, rank, 1)
        for side in range(2):
            index = 2 * pair + side
            place = place_ref[pl.ds(index * length, length), :]
            both = jnp.where(low, code, turned) if side == 0 else jnp.where(low, turned, code)
            spread = jnp.concatenate(
                [
                    jnp.where(part + group * per_group == place, both, 0.0).astype(jnp.bfloat16)
                    for group in range(width // LANES)
                ],
                axis=1,
            )
            out_refs[index][...] = jnp.dot(
                spread, store_ref[...], preferred_element_type=jnp.float32
            ).astype(jnp.bfloat16)


def expand(codes, places, store, rank, count):
    width, features = store.shape
    length = codes.shape[0] // (count // 2)
    block = min(512, features)
    whole = lambda array: pl.BlockSpec(array.shape, lambda i: (0, 0))
    return pl.pallas_call(
        functools.partial(expand_kernel, count, rank),
        grid=(features // block,),
        in_specs=[whole(places), whole(codes), pl.BlockSpec((width, block), lambda i: (0, i))],
        out_specs=[pl.BlockSpec((length, block), lambda i: (0, i))] * count,
        out_shape=[jax.ShapeDtypeStruct((length, features), jnp.bfloat16)] * count,
        compiler_params=pltpu.CompilerParams(
            dimension_semantics=("arbitrary",), vmem_limit_bytes=40 * 2**20
        ),
        cost_estimate=pl.CostEstimate(
            flops=2 * count * length * features * width,
            bytes_accessed=2 * features * (count * length + width),
            transcendentals=0,
        ),
        name="expand",
    )(places, codes, store)


def body(inputs, out_weight, shrink_store, expand_store, owner_map, requests, row_slot):
    steps_count, rows_count, feature_shard = inputs.shape
    stored, rank = shrink_store.shape[:2]
    slot_count = requests.shape[2]
    pool_size, tp_size = lax.axis_size("pool"), lax.axis_size("tp")
    chips = pool_size // 2
    my_pool, my_tp = lax.axis_index("pool"), lax.axis_index("tp")
    my_chip, my_core = my_pool // 2, my_pool % 2
    all_rows = steps_count * rows_count
    flat = inputs.reshape(all_rows, feature_shard)
    shrink_flat = shrink_store.reshape(stored * rank, feature_shard)
    expand_flat = expand_store.reshape(stored * rank, feature_shard)

    swap = [(p, p ^ 1) for p in range(pool_size)]
    shift = lambda k: [(p, (p // 2 + k) % chips * 2 + p % 2) for p in range(pool_size)]
    around = [(i, (i + 1) % tp_size) for i in range(tp_size)]

    per_half = all_rows // HALVES
    halves = [flat[h * per_half : (h + 1) * per_half] for h in range(HALVES)]

    mine = [[half] + [lax.ppermute(half, "pool", shift(k)) for k in range(1, chips)] for half in halves]
    theirs = [[lax.ppermute(part, "pool", swap) for part in group] for group in mine]

    ids = jnp.arange(owner_map.shape[0], dtype=jnp.int32)
    positions = jnp.sum(
        jnp.where(requests[:, 0, :, None] == ids, owner_map, 0), axis=-1
    )
    slots = jnp.arange(slot_count, dtype=jnp.int32)
    row_position = jnp.sum(
        jnp.where(row_slot[:, :, None] == slots, positions[:, None, :], 0), axis=-1
    )
    every = lax.all_gather(row_position.reshape(1, all_rows), "pool", axis=0, tiled=True)
    every = every - my_pool * stored

    def places(h):
        found = []
        for core in (my_core, 1 - my_core):
            for k in range(chips):
                source = (my_chip - k + chips) % chips * 2 + core
                found.append(
                    lax.dynamic_slice(every, (source, h * per_half), (1, per_half))[0]
                )
        return jnp.broadcast_to(jnp.concatenate(found)[:, None], (pool_size * per_half, LANES))

    def base_part(back):
        target = (my_tp - back + tp_size) % tp_size
        columns = lax.dynamic_slice(
            out_weight, (0, target * feature_shard), (out_weight.shape[0], feature_shard)
        )
        return jnp.dot(flat, columns, preferred_element_type=jnp.float32)

    cut = lambda array, s: array[s * rows_count : (s + 1) * rows_count]
    part = base_part(1)
    moving = [cut(part, s).astype(jnp.bfloat16) for s in range(steps_count)]
    for back in range(2, tp_size + 1):
        part = base_part(back)
        moving = [
            cut(part, s) + lax.ppermute(moving[s], "tp", around).astype(jnp.float32)
            for s in range(steps_count)
        ]
        if back < tp_size:
            moving = [m.astype(jnp.bfloat16) for m in moving]

    updates = []
    for h in range(HALVES):
        place = places(h)
        codes = shrink(mine[h] + theirs[h], place, shrink_flat, rank)
        codes = lax.psum(codes, "tp")
        terms = expand(codes, place, expand_flat, rank, pool_size)
        total = None
        for k in range(chips):
            joined = terms[k] + lax.ppermute(terms[chips + k], "pool", swap)
            if k > 0:
                joined = lax.ppermute(joined, "pool", shift(chips - k))
            total = joined if total is None else total + joined
        updates.append(total)

    per = steps_count // HALVES
    rows_out = [
        (
            moving[s]
            + adapter_scale * cut(updates[s // per], s % per).astype(jnp.float32)
        ).astype(jnp.bfloat16)
        for s in range(steps_count)
    ]
    return jnp.stack(rows_out, axis=0)


def solution(mesh):
    placed = (
        P(None, ("groups", "pool"), "tp"),
        P("tp", None),
        P(("groups", "pool"), None, "tp"),
        P(("groups", "pool"), None, "tp"),
        P("groups"),
        P(None, ("groups", "pool"), None),
        P(None, ("groups", "pool")),
    )
    return jax.shard_map(
        body,
        mesh=mesh,
        in_specs=placed,
        out_specs=P(None, ("groups", "pool"), "tp"),
        check_vma=False,
    )
```

```python
import functools

import jax
import jax.numpy as jnp
from jax import lax
from jax.experimental import pallas as pl
from jax.experimental.pallas import tpu as pltpu
from jax.sharding import PartitionSpec as P

adapter_scale = 2.0
LANES = 128
HALVES = 2


def lane_parts(shape, rank):
    lane = lax.broadcasted_iota(jnp.int32, shape, 1)
    return lane // rank, lane < rank


def shrink_kernel(count, rank, *refs):
    rows_refs = refs[:count]
    place_ref, store_ref, _, out_ref = refs[count:]
    block = store_ref.shape[0]
    length = rows_refs[0].shape[0]
    step = pl.program_id(0)
    part, low = lane_parts((length, LANES), rank)
    per_group = LANES // rank
    first = step * (block // rank)
    for pair in range(count // 2):
        folded = []
        for side in range(2):
            index = 2 * pair + side
            place = place_ref[pl.ds(index * length, length), :] - first
            codes = lax.dot_general(
                rows_refs[index][...],
                store_ref[...],
                (((1,), (1,)), ((), ())),
                preferred_element_type=jnp.float32,
            )
            picked = jnp.zeros((length, LANES), jnp.float32)
            for group in range(block // LANES):
                picked += jnp.where(
                    part + group * per_group == place,
                    codes[:, group * LANES : (group + 1) * LANES],
                    0.0,
                )
            folded.append(picked + pltpu.roll(picked, rank, 1))
        packed = jnp.where(low, folded[0], folded[1])
        where_to = pl.ds(pair * length, length)

        @pl.when(step == 0)
        def _():
            out_ref[where_to, :] = packed

        @pl.when(step > 0)
        def _():
            out_ref[where_to, :] += packed


def rows_block(length, features, index):
    return pl.BlockSpec((length, features), lambda i: (index, 0))


def shrink(rows, length, places, store, rank, token):
    count, features = len(rows), store.shape[1]
    width = store.shape[0]
    block = min(256, width)
    whole = lambda array: pl.BlockSpec(array.shape, lambda i: (0, 0))
    out = jax.ShapeDtypeStruct((count // 2 * length, LANES), jnp.float32)
    return pl.pallas_call(
        functools.partial(shrink_kernel, count, rank),
        grid=(width // block,),
        in_specs=[rows_block(length, features, index) for _, index in rows]
        + [
            whole(places),
            pl.BlockSpec((block, features), lambda i: (i, 0)),
            pl.BlockSpec(memory_space=pl.ANY),
        ],
        out_specs=whole(out),
        out_shape=out,
        compiler_params=pltpu.CompilerParams(
            dimension_semantics=("arbitrary",), vmem_limit_bytes=40 * 2**20
        ),
        cost_estimate=pl.CostEstimate(
            flops=count * length,
            bytes_accessed=count * length,
            transcendentals=0,
        ),
        name="shrink",
    )(*[array for array, _ in rows], places, store, token)


def expand_kernel(count, rank, place_ref, code_ref, store_ref, _, *out_refs):
    width = store_ref.shape[0]
    length = out_refs[0].shape[0]
    part, low = lane_parts((length, LANES), rank)
    per_group = LANES // rank
    for pair in range(count // 2):
        code = code_ref[pl.ds(pair * length, length), :].astype(jnp.bfloat16).astype(jnp.float32)
        turned = pltpu.roll(code, rank, 1)
        for side in range(2):
            index = 2 * pair + side
            place = place_ref[pl.ds(index * length, length), :]
            both = jnp.where(low, code, turned) if side == 0 else jnp.where(low, turned, code)
            spread = jnp.concatenate(
                [
                    jnp.where(part + group * per_group == place, both, 0.0).astype(jnp.bfloat16)
                    for group in range(width // LANES)
                ],
                axis=1,
            )
            out_refs[index][...] = jnp.dot(
                spread, store_ref[...], preferred_element_type=jnp.float32
            ).astype(jnp.bfloat16)


def expand(codes, places, store, rank, count, token):
    width, features = store.shape
    length = codes.shape[0] // (count // 2)
    block = min(512, features)
    whole = lambda array: pl.BlockSpec(array.shape, lambda i: (0, 0))
    return pl.pallas_call(
        functools.partial(expand_kernel, count, rank),
        grid=(features // block,),
        in_specs=[
            whole(places),
            whole(codes),
            pl.BlockSpec((width, block), lambda i: (0, i)),
            pl.BlockSpec(memory_space=pl.ANY),
        ],
        out_specs=[pl.BlockSpec((length, block), lambda i: (0, i))] * count,
        out_shape=[jax.ShapeDtypeStruct((length, features), jnp.bfloat16)] * count,
        compiler_params=pltpu.CompilerParams(
            dimension_semantics=("arbitrary",), vmem_limit_bytes=40 * 2**20
        ),
        cost_estimate=pl.CostEstimate(
            flops=count * length,
            bytes_accessed=count * length,
            transcendentals=0,
        ),
        name="expand",
    )(places, codes, store, token)


def add_kernel(part_ref, moving_ref, _, out_ref):
    out_ref[...] = (part_ref[...] + moving_ref[...].astype(jnp.float32)).astype(jnp.bfloat16)


def add(part, moving, chunk, token):
    length, features = moving.shape
    pieces = 4
    block = (length // pieces, features)
    return pl.pallas_call(
        add_kernel,
        grid=(pieces,),
        in_specs=[
            pl.BlockSpec(block, lambda i: (chunk * pieces + i, 0)),
            pl.BlockSpec(block, lambda i: (i, 0)),
            pl.BlockSpec(memory_space=pl.ANY),
        ],
        out_specs=pl.BlockSpec(block, lambda i: (i, 0)),
        out_shape=jax.ShapeDtypeStruct((length, features), jnp.bfloat16),
        compiler_params=pltpu.CompilerParams(
            dimension_semantics=("arbitrary",), vmem_limit_bytes=16 * 2**20
        ),
        cost_estimate=pl.CostEstimate(
            flops=length, bytes_accessed=length, transcendentals=0
        ),
        name="add",
    )(part, moving, token)


def body(inputs, out_weight, shrink_store, expand_store, owner_map, requests, row_slot):
    steps_count, rows_count, feature_shard = inputs.shape
    stored, rank = shrink_store.shape[:2]
    slot_count = requests.shape[2]
    pool_size, tp_size = lax.axis_size("pool"), lax.axis_size("tp")
    chips = pool_size // 2
    my_pool, my_tp = lax.axis_index("pool"), lax.axis_index("tp")
    my_chip, my_core = my_pool // 2, my_pool % 2
    all_rows = steps_count * rows_count
    flat = inputs.reshape(all_rows, feature_shard)
    shrink_flat = shrink_store.reshape(stored * rank, feature_shard)
    expand_flat = expand_store.reshape(stored * rank, feature_shard)

    swap = [(p, p ^ 1) for p in range(pool_size)]
    shift = lambda k: [(p, (p // 2 + k) % chips * 2 + p % 2) for p in range(pool_size)]
    around = [(i, (i + 1) % tp_size) for i in range(tp_size)]

    per_half = all_rows // HALVES
    halves = [flat[h * per_half : (h + 1) * per_half] for h in range(HALVES)]

    far = [[lax.ppermute(half, "pool", shift(k)) for k in range(1, chips)] for half in halves]
    near = lax.ppermute(flat, "pool", swap)
    far_near = [[lax.ppermute(part, "pool", swap) for part in group] for group in far]

    def rows_of(h):
        first = [(flat, h)] + [(part, 0) for part in far[h]]
        return first + [(near, h)] + [(part, 0) for part in far_near[h]]

    ids = jnp.arange(owner_map.shape[0], dtype=jnp.int32)
    positions = jnp.sum(
        jnp.where(requests[:, 0, :, None] == ids, owner_map, 0), axis=-1
    )
    slots = jnp.arange(slot_count, dtype=jnp.int32)
    row_position = jnp.sum(
        jnp.where(row_slot[:, :, None] == slots, positions[:, None, :], 0), axis=-1
    )
    every = lax.all_gather(row_position.reshape(1, all_rows), "pool", axis=0, tiled=True)
    every = every - my_pool * stored

    def places(h):
        found = []
        for core in (my_core, 1 - my_core):
            for k in range(chips):
                source = (my_chip - k + chips) % chips * 2 + core
                found.append(
                    lax.dynamic_slice(every, (source, h * per_half), (1, per_half))[0]
                )
        return jnp.broadcast_to(jnp.concatenate(found)[:, None], (pool_size * per_half, LANES))

    def base_part(back):
        target = (my_tp - back + tp_size) % tp_size
        columns = lax.dynamic_slice(
            out_weight, (0, target * feature_shard), (out_weight.shape[0], feature_shard)
        )
        return jnp.dot(flat, columns, preferred_element_type=jnp.float32)

    cut = lambda array, h: array[h * per_half : (h + 1) * per_half]
    parts = [base_part(back) for back in range(1, tp_size + 1)]
    moving = [cut(parts[0], h).astype(jnp.bfloat16) for h in range(HALVES)]

    def ring(back, h, token):
        arrived = lax.ppermute(moving[h], "tp", around)
        moving[h] = add(parts[back - 1], arrived, h, token)
        return moving[h]

    def update_of(terms):
        total = last = None
        for k in range(chips):
            joined = terms[k] + lax.ppermute(terms[chips + k], "pool", swap)
            if k > 0:
                last = joined
                joined = lax.ppermute(joined, "pool", shift(chips - k))
            total = joined if total is None else total + joined
        return total, last

    place = [places(h) for h in range(HALVES)]
    token = moving[0]
    codes = [None] * HALVES
    steps = [(back, h) for back in range(2, tp_size) for h in range(HALVES)]
    for h in range(HALVES):
        codes[h] = token = shrink(rows_of(h), per_half, place[h], shrink_flat, rank, token)
        if h > 0:
            codes[h], _ = lax.optimization_barrier((codes[h], codes[h - 1]))
        codes[h] = lax.psum(codes[h], "tp")
        token = ring(*steps.pop(0), token)
    updates = []
    for h in range(HALVES):
        terms = expand(codes[h], place[h], expand_flat, rank, pool_size, token)
        update, token = update_of(terms)
        updates.append(update)
        if h == 0:
            for _ in range(HALVES):
                token = ring(*steps.pop(0), token)
    for back, h in steps:
        token = ring(back, h, token)

    rows_out = []
    for h in range(HALVES):
        base = cut(parts[-1], h) + lax.ppermute(moving[h], "tp", around).astype(jnp.float32)
        update = updates[h].astype(jnp.float32)
        rows_out.append((base + adapter_scale * update).astype(jnp.bfloat16))
    return jnp.concatenate(rows_out, axis=0).reshape(inputs.shape)


def solution(mesh):
    placed = (
        P(None, ("groups", "pool"), "tp"),
        P("tp", None),
        P(("groups", "pool"), None, "tp"),
        P(("groups", "pool"), None, "tp"),
        P("groups"),
        P(None, ("groups", "pool"), None),
        P(None, ("groups", "pool")),
    )
    return jax.shard_map(
        body,
        mesh=mesh,
        in_specs=placed,
        out_specs=P(None, ("groups", "pool"), "tp"),
        check_vma=False,
    )
```

```python
import functools

import jax
import jax.numpy as jnp
from jax import lax
from jax.experimental import pallas as pl
from jax.experimental.pallas import tpu as pltpu
from jax.sharding import PartitionSpec as P

adapter_scale = 2.0
LANES = 128
HALVES = 2


def lane_parts(shape, rank):
    lane = lax.broadcasted_iota(jnp.int32, shape, 1)
    return lane // rank, lane < rank


def shrink_kernel(count, rank, *refs):
    rows_refs = refs[:count]
    place_ref, store_ref, out_ref = refs[count:]
    block = store_ref.shape[0]
    length = rows_refs[0].shape[0]
    step = pl.program_id(0)
    part, low = lane_parts((length, LANES), rank)
    per_group = LANES // rank
    first = step * (block // rank)
    for pair in range(count // 2):
        folded = []
        for side in range(2):
            index = 2 * pair + side
            place = place_ref[pl.ds(index * length, length), :] - first
            codes = lax.dot_general(
                rows_refs[index][...],
                store_ref[...],
                (((1,), (1,)), ((), ())),
                preferred_element_type=jnp.float32,
            )
            picked = jnp.zeros((length, LANES), jnp.float32)
            for group in range(block // LANES):
                picked += jnp.where(
                    part + group * per_group == place,
                    codes[:, group * LANES : (group + 1) * LANES],
                    0.0,
                )
            folded.append(picked + pltpu.roll(picked, rank, 1))
        packed = jnp.where(low, folded[0], folded[1])
        where_to = pl.ds(pair * length, length)

        @pl.when(step == 0)
        def _():
            out_ref[where_to, :] = packed

        @pl.when(step > 0)
        def _():
            out_ref[where_to, :] += packed


def shrink(rows, places, store, rank):
    count, (length, features) = len(rows), rows[0].shape
    width = store.shape[0]
    block = min(256, width)
    whole = lambda array: pl.BlockSpec(array.shape, lambda i: (0, 0))
    out = jax.ShapeDtypeStruct((count // 2 * length, LANES), jnp.float32)
    return pl.pallas_call(
        functools.partial(shrink_kernel, count, rank),
        grid=(width // block,),
        in_specs=[whole(r) for r in rows]
        + [whole(places), pl.BlockSpec((block, features), lambda i: (i, 0))],
        out_specs=whole(out),
        out_shape=out,
        compiler_params=pltpu.CompilerParams(
            dimension_semantics=("arbitrary",), vmem_limit_bytes=40 * 2**20
        ),
        cost_estimate=pl.CostEstimate(
            flops=2 * count * length * features * width,
            bytes_accessed=2 * features * (count * length + width),
            transcendentals=0,
        ),
        name="shrink",
    )(*rows, places, store)


def expand_kernel(count, rank, place_ref, code_ref, store_ref, *out_refs):
    width = store_ref.shape[0]
    length = out_refs[0].shape[0]
    part, low = lane_parts((length, LANES), rank)
    per_group = LANES // rank
    for pair in range(count // 2):
        code = code_ref[pl.ds(pair * length, length), :].astype(jnp.bfloat16).astype(jnp.float32)
        turned = pltpu.roll(code, rank, 1)
        for side in range(2):
            index = 2 * pair + side
            place = place_ref[pl.ds(index * length, length), :]
            both = jnp.where(low, code, turned) if side == 0 else jnp.where(low, turned, code)
            spread = jnp.concatenate(
                [
                    jnp.where(part + group * per_group == place, both, 0.0).astype(jnp.bfloat16)
                    for group in range(width // LANES)
                ],
                axis=1,
            )
            out_refs[index][...] = jnp.dot(
                spread, store_ref[...], preferred_element_type=jnp.float32
            ).astype(jnp.bfloat16)


def expand(codes, places, store, rank, count):
    width, features = store.shape
    length = codes.shape[0] // (count // 2)
    block = min(512, features)
    whole = lambda array: pl.BlockSpec(array.shape, lambda i: (0, 0))
    return pl.pallas_call(
        functools.partial(expand_kernel, count, rank),
        grid=(features // block,),
        in_specs=[whole(places), whole(codes), pl.BlockSpec((width, block), lambda i: (0, i))],
        out_specs=[pl.BlockSpec((length, block), lambda i: (0, i))] * count,
        out_shape=[jax.ShapeDtypeStruct((length, features), jnp.bfloat16)] * count,
        compiler_params=pltpu.CompilerParams(
            dimension_semantics=("arbitrary",), vmem_limit_bytes=40 * 2**20
        ),
        cost_estimate=pl.CostEstimate(
            flops=2 * count * length * features * width,
            bytes_accessed=2 * features * (count * length + width),
            transcendentals=0,
        ),
        name="expand",
    )(places, codes, store)


def body(inputs, out_weight, shrink_store, expand_store, owner_map, requests, row_slot):
    steps_count, rows_count, feature_shard = inputs.shape
    stored, rank = shrink_store.shape[:2]
    slot_count = requests.shape[2]
    pool_size = lax.axis_size("pool")
    chips = pool_size // 2
    my_pool = lax.axis_index("pool")
    my_chip, my_core = my_pool // 2, my_pool % 2
    all_rows = steps_count * rows_count
    flat = inputs.reshape(all_rows, feature_shard)
    shrink_flat = shrink_store.reshape(stored * rank, feature_shard)
    expand_flat = expand_store.reshape(stored * rank, feature_shard)

    swap = [(p, p ^ 1) for p in range(pool_size)]
    shift = lambda k: [(p, (p // 2 + k) % chips * 2 + p % 2) for p in range(pool_size)]

    ids = jnp.arange(owner_map.shape[0], dtype=jnp.int32)
    positions = jnp.sum(
        jnp.where(requests[:, 0, :, None] == ids, owner_map, 0), axis=-1
    )
    slots = jnp.arange(slot_count, dtype=jnp.int32)
    row_position = jnp.sum(
        jnp.where(row_slot[:, :, None] == slots, positions[:, None, :], 0), axis=-1
    )
    every = lax.all_gather(row_position.reshape(1, all_rows), "pool", axis=0, tiled=True)
    every, flat_sent = lax.optimization_barrier((every, flat))
    every = every - my_pool * stored

    per_half = all_rows // HALVES
    halves = [flat_sent[h * per_half : (h + 1) * per_half] for h in range(HALVES)]

    mine = [[half] + [lax.ppermute(half, "pool", shift(k)) for k in range(1, chips)] for half in halves]
    theirs = [[lax.ppermute(part, "pool", swap) for part in group] for group in mine]

    def places(h, every):
        found = []
        for core in (my_core, 1 - my_core):
            for k in range(chips):
                source = (my_chip - k + chips) % chips * 2 + core
                found.append(
                    lax.dynamic_slice(every, (source, h * per_half), (1, per_half))[0]
                )
        return jnp.broadcast_to(jnp.concatenate(found)[:, None], (pool_size * per_half, LANES))

    def partial_of(rows):
        return lax.dot_general(
            out_weight, rows, (((0,), (1,)), ((), ())), preferred_element_type=jnp.float32
        ).astype(jnp.bfloat16)

    def base_of(partial):
        return lax.psum_scatter(partial, "tp", scatter_dimension=0, tiled=True)

    cut = lambda array, s: array[s * rows_count : (s + 1) * rows_count]
    early = [partial_of(cut(flat, s)) for s in range(steps_count // HALVES)]
    bases = [base_of(partial) for partial in early]
    every, *_ = lax.optimization_barrier((every, *early))
    place = [places(h, every) for h in range(HALVES)]
    codes = [shrink(mine[h] + theirs[h], place[h], shrink_flat, rank) for h in range(HALVES)]
    later, *codes = lax.optimization_barrier((flat[steps_count // HALVES * rows_count :], *codes))
    partial, bases, codes = lax.optimization_barrier((partial_of(later), bases, codes))
    codes = lax.psum(codes, "tp")
    bases = [base.T for base in [*bases, base_of(partial)]]
    moving = jnp.concatenate(bases, axis=0).astype(jnp.float32)

    updates = []
    for h in range(HALVES):
        terms = expand(codes[h], place[h], expand_flat, rank, pool_size)
        total = None
        for k in range(chips):
            joined = terms[k] + lax.ppermute(terms[chips + k], "pool", swap)
            if k > 0:
                joined = lax.ppermute(joined, "pool", shift(chips - k))
            total = joined if total is None else total + joined
        updates.append(total)

    update = jnp.concatenate(updates, axis=0).astype(jnp.float32)
    return (moving + adapter_scale * update).astype(jnp.bfloat16).reshape(inputs.shape)


def solution(mesh):
    placed = (
        P(None, ("groups", "pool"), "tp"),
        P("tp", None),
        P(("groups", "pool"), None, "tp"),
        P(("groups", "pool"), None, "tp"),
        P("groups"),
        P(None, ("groups", "pool"), None),
        P(None, ("groups", "pool")),
    )
    return jax.shard_map(
        body,
        mesh=mesh,
        in_specs=placed,
        out_specs=P(None, ("groups", "pool"), "tp"),
        check_vma=False,
    )
```

```python
import functools

import jax
import jax.numpy as jnp
from jax import lax
from jax.experimental import pallas as pl
from jax.experimental.pallas import tpu as pltpu
from jax.sharding import PartitionSpec as P

adapter_scale = 2.0
LANES = 128
HALVES = 2


def lane_parts(shape, rank):
    lane = lax.broadcasted_iota(jnp.int32, shape, 1)
    return lane // rank, lane < rank


def shrink_kernel(count, rank, *refs):
    rows_refs = refs[:count]
    place_ref, store_ref, out_ref = refs[count:]
    block = store_ref.shape[0]
    length = rows_refs[0].shape[0]
    step = pl.program_id(0)
    part, low = lane_parts((length, LANES), rank)
    per_group = LANES // rank
    first = step * (block // rank)
    for pair in range(count // 2):
        folded = []
        for side in range(2):
            index = 2 * pair + side
            place = place_ref[pl.ds(index * length, length), :] - first
            codes = lax.dot_general(
                rows_refs[index][...],
                store_ref[...],
                (((1,), (1,)), ((), ())),
                preferred_element_type=jnp.float32,
            )
            picked = jnp.zeros((length, LANES), jnp.float32)
            for group in range(block // LANES):
                picked += jnp.where(
                    part + group * per_group == place,
                    codes[:, group * LANES : (group + 1) * LANES],
                    0.0,
                )
            folded.append(picked + pltpu.roll(picked, rank, 1))
        packed = jnp.where(low, folded[0], folded[1])
        where_to = pl.ds(pair * length, length)

        @pl.when(step == 0)
        def _():
            out_ref[where_to, :] = packed

        @pl.when(step > 0)
        def _():
            out_ref[where_to, :] += packed


def shrink(rows, places, store, rank):
    count, (length, features) = len(rows), rows[0].shape
    width = store.shape[0]
    block = min(256, width)
    whole = lambda array: pl.BlockSpec(array.shape, lambda i: (0, 0))
    out = jax.ShapeDtypeStruct((count // 2 * length, LANES), jnp.float32)
    return pl.pallas_call(
        functools.partial(shrink_kernel, count, rank),
        grid=(width // block,),
        in_specs=[whole(r) for r in rows]
        + [whole(places), pl.BlockSpec((block, features), lambda i: (i, 0))],
        out_specs=whole(out),
        out_shape=out,
        compiler_params=pltpu.CompilerParams(
            dimension_semantics=("arbitrary",), vmem_limit_bytes=40 * 2**20
        ),
        cost_estimate=pl.CostEstimate(
            flops=2 * count * length * features * width,
            bytes_accessed=2 * features * (count * length + width),
            transcendentals=0,
        ),
        name="shrink",
    )(*rows, places, store)


def expand_kernel(count, rank, place_ref, code_ref, store_ref, *out_refs):
    width = store_ref.shape[0]
    length = out_refs[0].shape[0]
    part, low = lane_parts((length, LANES), rank)
    per_group = LANES // rank
    for pair in range(count // 2):
        code = code_ref[pl.ds(pair * length, length), :].astype(jnp.bfloat16).astype(jnp.float32)
        turned = pltpu.roll(code, rank, 1)
        for side in range(2):
            index = 2 * pair + side
            place = place_ref[pl.ds(index * length, length), :]
            both = jnp.where(low, code, turned) if side == 0 else jnp.where(low, turned, code)
            spread = jnp.concatenate(
                [
                    jnp.where(part + group * per_group == place, both, 0.0).astype(jnp.bfloat16)
                    for group in range(width // LANES)
                ],
                axis=1,
            )
            out_refs[index][...] = jnp.dot(
                spread, store_ref[...], preferred_element_type=jnp.float32
            ).astype(jnp.bfloat16)


def expand(codes, places, store, rank, count):
    width, features = store.shape
    length = codes.shape[0] // (count // 2)
    block = min(512, features)
    whole = lambda array: pl.BlockSpec(array.shape, lambda i: (0, 0))
    return pl.pallas_call(
        functools.partial(expand_kernel, count, rank),
        grid=(features // block,),
        in_specs=[whole(places), whole(codes), pl.BlockSpec((width, block), lambda i: (0, i))],
        out_specs=[pl.BlockSpec((length, block), lambda i: (0, i))] * count,
        out_shape=[jax.ShapeDtypeStruct((length, features), jnp.bfloat16)] * count,
        compiler_params=pltpu.CompilerParams(
            dimension_semantics=("arbitrary",), vmem_limit_bytes=40 * 2**20
        ),
        cost_estimate=pl.CostEstimate(
            flops=2 * count * length * features * width,
            bytes_accessed=2 * features * (count * length + width),
            transcendentals=0,
        ),
        name="expand",
    )(places, codes, store)


def body(inputs, out_weight, shrink_store, expand_store, owner_map, requests, row_slot):
    steps_count, rows_count, feature_shard = inputs.shape
    stored, rank = shrink_store.shape[:2]
    slot_count = requests.shape[2]
    pool_size, tp_size = lax.axis_size("pool"), lax.axis_size("tp")
    chips = pool_size // 2
    my_pool, my_tp = lax.axis_index("pool"), lax.axis_index("tp")
    all_rows = steps_count * rows_count
    flat = inputs.reshape(all_rows, feature_shard)
    shrink_flat = shrink_store.reshape(stored * rank, feature_shard)
    expand_flat = expand_store.reshape(stored * rank, feature_shard)

    swap = [(p, p ^ 1) for p in range(pool_size)]
    shift = lambda k: [(p, (p // 2 + k) % chips * 2 + p % 2) for p in range(pool_size)]

    ids = jnp.arange(owner_map.shape[0], dtype=jnp.int32)
    positions = jnp.sum(
        jnp.where(requests[:, 0, :, None] == ids, owner_map, 0), axis=-1
    )
    slots = jnp.arange(slot_count, dtype=jnp.int32)
    row_position = jnp.sum(
        jnp.where(row_slot[:, :, None] == slots, positions[:, None, :], 0), axis=-1
    )
    own = row_position.reshape(1, all_rows)
    same_core = jnp.concatenate(
        [own] + [lax.ppermute(own, "pool", shift(k)) for k in range(1, chips)], axis=0
    )
    every = jnp.concatenate([same_core, lax.ppermute(same_core, "pool", swap)], axis=0)
    every = every - my_pool * stored

    per_half = all_rows // HALVES
    halves = [flat[h * per_half : (h + 1) * per_half] for h in range(HALVES)]

    mine = [[half] + [lax.ppermute(half, "pool", shift(k)) for k in range(1, chips)] for half in halves]
    theirs = [[lax.ppermute(part, "pool", swap) for part in group] for group in mine]

    def places(h, every):
        found = every[:, h * per_half : (h + 1) * per_half].reshape(pool_size * per_half, 1)
        return jnp.broadcast_to(found, (pool_size * per_half, LANES))

    def code_sum(codes):
        codes = codes.reshape(tp_size, -1, LANES)
        turn = lambda k: [(i, (i + k) % tp_size) for i in range(tp_size)]
        part = lambda index: lax.dynamic_index_in_dim(codes, index % tp_size, 0, False)
        total = part(my_tp)
        for k in range(1, tp_size):
            total = total + lax.ppermute(part(my_tp + k), "tp", turn(k))
        total = total.astype(jnp.bfloat16)
        whole = jnp.zeros(codes.shape, jnp.bfloat16)
        whole = lax.dynamic_update_index_in_dim(whole, total, my_tp, 0)
        for k in range(1, tp_size):
            other = lax.ppermute(total, "tp", turn(k))
            whole = lax.dynamic_update_index_in_dim(
                whole, other, (my_tp - k + tp_size) % tp_size, 0
            )
        return whole.reshape(-1, LANES)

    def partial_of(rows):
        return lax.dot_general(
            out_weight, rows, (((0,), (1,)), ((), ())), preferred_element_type=jnp.float32
        ).astype(jnp.bfloat16)

    def base_of(partial):
        return lax.psum_scatter(partial, "tp", scatter_dimension=0, tiled=True)

    cut = lambda array, s: array[s * rows_count : (s + 1) * rows_count]
    first = steps_count // HALVES
    groups = [cut(flat, s) for s in range(first)] + [flat[first * rows_count :]]
    partials = [partial_of(rows) for rows in groups]
    bases = [base_of(partial) for partial in partials]
    every, *_ = lax.optimization_barrier((every, *partials))
    place = [places(h, every) for h in range(HALVES)]
    codes = [shrink(mine[h] + theirs[h], place[h], shrink_flat, rank) for h in range(HALVES)]
    codes = jnp.concatenate(codes, axis=0)
    codes, bases[0] = lax.optimization_barrier((codes, bases[0]))
    codes, *bases[1:first] = lax.optimization_barrier((code_sum(codes), *bases[1:first]))
    codes = jnp.split(codes, HALVES, axis=0)
    bases = [base.T for base in bases]
    moving = jnp.concatenate(bases, axis=0).astype(jnp.float32)

    updates = []
    for h in range(HALVES):
        terms = expand(codes[h], place[h], expand_flat, rank, pool_size)
        total = None
        for k in range(chips):
            joined = terms[k] + lax.ppermute(terms[chips + k], "pool", swap)
            if k > 0:
                joined = lax.ppermute(joined, "pool", shift(chips - k))
            total = joined if total is None else total + joined
        updates.append(total)

    update = jnp.concatenate(updates, axis=0).astype(jnp.float32)
    return (moving + adapter_scale * update).astype(jnp.bfloat16).reshape(inputs.shape)


def solution(mesh):
    placed = (
        P(None, ("groups", "pool"), "tp"),
        P("tp", None),
        P(("groups", "pool"), None, "tp"),
        P(("groups", "pool"), None, "tp"),
        P("groups"),
        P(None, ("groups", "pool"), None),
        P(None, ("groups", "pool")),
    )
    return jax.shard_map(
        body,
        mesh=mesh,
        in_specs=placed,
        out_specs=P(None, ("groups", "pool"), "tp"),
        check_vma=False,
    )
```
